32 devices in a mesh: grp: 4 (over z), dev: 8 (over y, x, core).
Axes of the slice: x: 2, y: 2, z: 4, core: 2. Of those that a mesh axis runs over, the one named last changes fastest.
Arguments:
- rhs: float32 [2048, 64, 128], P(('grp', 'dev')), may hold values from -6 to 6
- jacobian: bfloat16 [2048, 7, 128, 128], P(('grp', 'dev'))
- columns: int32 [2048, 7], P(('grp', 'dev')), may hold values from 0 to 95, as said below
- send_tiles: int32 [32, 4, 8], P(('grp', 'dev')), may hold values from 0 to 63
- smoother: bfloat16 [2048, 128, 128], P(('grp', 'dev'))
- restriction: bfloat16 [2048, 128, 128], P(('grp', 'dev')), may hold values from -0.25 to 0.25
- coarse_inverse: bfloat16 [8, 8, 8, 128, 128], P('dev')
- owner: int32 [256, 1], replicated, may hold values from 0 to 7; in each aligned block of 32 rows (0 to 31, 32 to 63, ...) at most 8 rows name the same one
Outputs:
- correction: float32 [2048, 64, 128], P(('grp', 'dev'))
The draws below stay inside these ranges and needn't reach their ends.
Inputs may be any that keep to these rules, and one draw needn't show every extreme that they name: columns[n, 0] is the local index t of tile n itself; columns[n, 1] and columns[n, 2] are below 64; columns[n, 3 + j] lies in 64 + j * 8 to 64 + (j + 1) * 8 - 1. In each aligned block of 32 rows (the coarse blocks of one domain position) no owner is named more than 8 times.
All inputs are finite; a program needn't handle non-finite values.
Results may differ from the reference program's by a relative error of at most 0.0035.
Values may be sent and summed in bfloat16 or wider, within the bound.
A program may use at most 128 MiB of HBM per device.

```python
import math
import jax
import jax.numpy as jnp
import numpy as np
from jax import lax

R = 128
K = 7
AGG = 2
SWEEPS = 3
NRHS = 64
TPD = 64
SUBS = 4
DOMS = 8
HB = 8
CPD = 32
CAP = 8
COARSE = 256
TILES = 2048


def draw_jacobian(key, part):
    shape = (TILES, K, R, R)
    base = jax.random.normal(key, shape, jnp.float32)
    first = (jnp.arange(K) == 0).astype(jnp.float32)
    scale = (0.15 + 0.45 * first) / math.sqrt(R)
    diagonal = 2.0 * first[:, None, None] * jnp.eye(R, dtype=jnp.float32)[None]
    return (base * scale[None, :, None, None] + diagonal[None]).astype(jnp.bfloat16)


def draw_columns(key, part):
    key_local, key_halo = jax.random.split(jax.random.fold_in(key, 11))
    local = jax.random.randint(key_local, (TILES, 2), 0, TPD)
    halo = jax.random.randint(key_halo, (TILES, 4), 0, HB) + TPD + HB * jnp.arange(4, dtype=jnp.int32)[None, :]
    itself = jnp.arange(TILES, dtype=jnp.int32) % TPD
    return jnp.concatenate([itself[:, None], local, halo], axis=1).astype(jnp.int32)


def draw_smoother(key, part):
    shape = (TILES, R, R)
    base = jax.random.normal(key, shape, jnp.float32)
    return (0.3 * jnp.eye(R, dtype=jnp.float32)[None] + base * (0.12 / math.sqrt(R))).astype(jnp.bfloat16)


def draw_coarse_inverse(key, part):
    shape = (DOMS, DOMS, CAP, R, R)
    base = jax.random.normal(key, shape, jnp.float32)
    return (0.5 * jnp.eye(R, dtype=jnp.float32) + base * (0.2 / math.sqrt(R))).astype(jnp.bfloat16)


def with_ends(drawn, stream_key, least, high):
    dims = drawn.shape
    spot = [jax.random.randint(jax.random.fold_in(stream_key, axis), (), 0, dims[axis]) for axis in range(len(dims))]
    drawn = drawn.at[tuple(spot)].set(least)
    longest = dims.index(max(dims))
    spot[longest] = (spot[longest] + 1) % dims[longest]
    return drawn.at[tuple(spot)].set(high)


def shard_levels(rng, extent, shards, smallest, top_value):
    level = 1.0
    for position, shards_of in shards:
        heights = jax.random.uniform(jax.random.fold_in(jax.random.fold_in(rng, 6), position), (shards_of,), jnp.float32, smallest / len(shards), top_value / len(shards))
        level = level * jnp.repeat(jnp.exp(heights), extent[position] // shards_of).reshape((-1,) + (1,) * (len(extent) - 1 - position))
    return level


def shared_out(stream_key, own, number, rows, number_of, top, limit, lean):
    order = jax.random.permutation(stream_key, number_of)
    packed, usual = shares(number_of, rows * top, limit, lean, True), shares(number_of, rows * top, limit, lean, False)
    places = jnp.arange(number_of)

    def named(sizes, rotation):
        used = int((sizes > 0).sum())
        fixed = max(1, used // 4)
        shifted = fixed + (places - fixed + rotation * (used - fixed)) % max(1, number_of - fixed)
        return jnp.zeros((number_of,), jnp.int32).at[order[jnp.where(places < fixed, places, shifted)]].set(jnp.asarray(sizes, jnp.int32))

    sizes = jnp.where(number % 4 == 0, named(packed, number // 4), named(usual, number - number // 4 - 1))
    mixed = jax.random.permutation(jax.random.fold_in(own, 3), number_of)
    giver, taker = mixed[0:number_of // 2 * 2:2], mixed[1:number_of // 2 * 2:2]
    margin = jnp.minimum(sizes[giver] - 1, limit - sizes[taker]) // 2
    margin = jnp.where((giver == order[0]) | (taker == order[0]) | (sizes[taker] == 0), 0, jnp.maximum(margin, 0))
    shifted = jax.random.randint(jax.random.fold_in(own, 4), (number_of // 2,), 0, 1 << 20) % (margin + 1)
    sizes = sizes.at[giver].add(-shifted).at[taker].add(shifted)
    members = jnp.searchsorted(jnp.cumsum(sizes), jnp.arange(rows * top), side="right").astype(jnp.int32)
    listing = members.reshape(top, rows).T
    listing = listing[jax.random.permutation(jax.random.fold_in(own, 1), rows)]
    rotation = jax.random.randint(jax.random.fold_in(own, 2), (rows, 1), 0, top)
    return jnp.take_along_axis(listing, (jnp.arange(top)[None, :] + rotation) % top, axis=1)


def shares(number_of, total, most, skew, full):
    loads = [(1 << 20) // math.isqrt(rank ** skew) + 1 for rank in range(1, number_of + 1)]
    largest = most if full else min(most, max(-(-total // number_of), total * loads[0] // sum(loads)))
    least = 1 if total - largest >= number_of - 1 else 0
    given, rest = [largest] + [least] * (number_of - 1), total - largest - least * (number_of - 1)
    while rest > 0:
        movable = [i for i in range(1, number_of) if given[i] < largest] or [i for i in range(1, number_of) if given[i] < most]
        pool, remaining = sum([loads[i] for i in movable]), rest
        for i in movable:
            extra = min(most - given[i], max(1, remaining * loads[i] // pool), rest)
            given[i] = given[i] + extra
            rest = rest - extra
    return np.array(given)


def bell_draw(stream_key, dims, deviation, most, cuts=(), kind=jnp.bfloat16):
    array = deviation * jax.random.normal(stream_key, dims, jnp.float32)
    if cuts:
        array = array * shard_levels(stream_key, dims, cuts, -0.22, 0.18)
    return jnp.clip(array, -most, most).astype(kind)


def setup_inputs(seed: int = 0) -> dict:
    key_list = jax.random.split(jax.random.key(seed), 9)
    rhs = bell_draw(key_list[0], (TILES, NRHS, R), 1.0, 6.0, ((0, 32),), jnp.float32)
    jacobian = draw_jacobian(jax.random.fold_in(key_list[8], 71), 0)
    columns = draw_columns(jax.random.fold_in(key_list[8], 71), 0)
    send_tiles = with_ends(jax.random.randint(key_list[3], (SUBS * DOMS, 4, HB), 0, TPD), jax.random.fold_in(key_list[3], 1), 0, TPD - 1).astype(jnp.int32)
    smoother = draw_smoother(jax.random.fold_in(key_list[8], 71), 0)
    restriction = bell_draw(key_list[5], (TILES, R, R), (4 * R) ** -0.5, 0.25, ((0, 32),))
    coarse_inverse = draw_coarse_inverse(jax.random.fold_in(key_list[8], 71), 0)
    owner_keys = jax.random.split(jax.random.fold_in(key_list[7], 1), COARSE // CPD)
    owner_turns = jax.random.permutation(jax.random.fold_in(key_list[7], 3), COARSE // CPD)
    owner = jax.vmap(lambda own, number: shared_out(jax.random.fold_in(key_list[7], 2), own, number, CPD, DOMS, 1, CAP, 2))(owner_keys, owner_turns).reshape((COARSE, 1))
    return {"rhs": rhs, "jacobian": jacobian, "columns": columns, "send_tiles": send_tiles, "smoother": smoother, "restriction": restriction, "coarse_inverse": coarse_inverse, "owner": owner}


OMEGA = 0.8


def reference(rhs, jacobian, columns, send_tiles, smoother, restriction, coarse_inverse, owner):
    domains = SUBS * DOMS
    mats = jacobian.reshape(domains, TPD, K, R, R)
    cols = columns.reshape(domains, TPD, K)
    sends = send_tiles.reshape(SUBS, DOMS, 4, HB)
    smooth = smoother.reshape(domains, TPD, R, R)
    restrict = restriction.reshape(domains, TPD, R, R)
    target = rhs.reshape(domains, TPD, NRHS, R)
    pick = jax.vmap(jax.vmap(lambda table, index: table[index]))

    def extend(vector_bf):
        whole = vector_bf.reshape(SUBS, DOMS, TPD, NRHS, R)
        packs = [pick(whole, sends[:, :, j]) for j in range(4)]
        zero_dev = jnp.zeros_like(packs[0][:, :1])
        zero_grp = jnp.zeros_like(packs[2][:1])
        from_left = jnp.concatenate([zero_dev, packs[0][:, :-1]], axis=1)
        from_right = jnp.concatenate([packs[1][:, 1:], zero_dev], axis=1)
        from_low = jnp.concatenate([zero_grp, packs[2][:-1]], axis=0)
        from_high = jnp.concatenate([packs[3][1:], zero_grp], axis=0)
        joined = jnp.concatenate([whole, from_left, from_right, from_low, from_high], axis=2)
        return joined.reshape(domains, TPD + 4 * HB, NRHS, R)

    def operate(state):
        extended = extend(state.astype(jnp.bfloat16))

        def one_domain(pieces):
            tiles_here, cols_here, ext_here = pieces
            gathered = ext_here[cols_here]
            return jnp.einsum('tkij,tkrj->tri', tiles_here.astype(jnp.float32), gathered.astype(jnp.float32))

        return lax.map(one_domain, (mats, cols, extended))

    def tiles_apply(matrices, vectors, form):
        return lax.map(lambda pieces: jnp.einsum(form, pieces[0].astype(jnp.float32), pieces[1].astype(jnp.float32)), (matrices, vectors))

    def jacobi(vectors):
        return tiles_apply(smooth, vectors.astype(jnp.bfloat16), 'tij,trj->tri')

    state = OMEGA * jacobi(target)
    for sweep in range(SWEEPS - 1):
        state = state + OMEGA * jacobi(target - operate(state))
    residual = target - operate(state)
    restricted = tiles_apply(restrict, residual.astype(jnp.bfloat16), 'tij,trj->tri')
    coarse = restricted.reshape(SUBS, DOMS, CPD, AGG, NRHS, R).sum(axis=(0, 3))
    owners = owner[:, 0].reshape(DOMS, CPD)
    order = jnp.arange(CPD, dtype=jnp.int32)
    earlier = (owners[:, :, None] == owners[:, None, :]) & (order[None, None, :] < order[None, :, None])
    slot = jnp.sum(earlier.astype(jnp.int32), axis=2)
    source = jnp.broadcast_to(jnp.arange(DOMS, dtype=jnp.int32)[:, None], (DOMS, CPD))
    picked = coarse_inverse[owners, source, slot]
    coarse_fix = jnp.einsum('dcab,dcrb->dcra', picked.astype(jnp.float32), coarse.astype(jnp.bfloat16).astype(jnp.float32)).astype(jnp.bfloat16)
    fine_fix = jnp.repeat(coarse_fix, AGG, axis=1)
    fine_fix = jnp.broadcast_to(fine_fix[None], (SUBS, DOMS, TPD, NRHS, R)).reshape(domains, TPD, NRHS, R)
    state = state + tiles_apply(restrict, fine_fix, 'tji,trj->tri')
    for sweep in range(SWEEPS):
        state = state + OMEGA * jacobi(target - operate(state))
    return state.reshape(TILES, NRHS, R)
```

```python
import functools

import jax
import jax.numpy as jnp
from jax import lax
from jax.experimental import pallas as pl
from jax.experimental.pallas import tpu as pltpu
from jax.sharding import PartitionSpec as P

AGG = 2
SWEEPS = 3
OMEGA = 0.8
GROUP = 8
LAG = 3
MESH = pl.DeviceIdType.MESH
EXCHANGES = 2 * SWEEPS


def nt(left, right):
    return lax.dot_general(
        left, right, (((1,), (1,)), ((), ())), preferred_element_type=jnp.float32
    )


def wide(parts):
    return jnp.concatenate(parts, axis=1)


def kernel(sizes, *refs):
    grps, devs, cap = sizes
    cols, listed, owners = refs[:3]
    rhs_hbm, jac_hbm, smooth_hbm, rest_hbm, inv_hbm, out_hbm = refs[3:9]
    rhs, jac, smooth, rest, inv = refs[9:14]
    x, acc, u, pack, own, low, high, up, down, pick = refs[14:24]
    halos = refs[24 : 24 + 4 * EXCHANGES]
    (rhs_sem, jac_sem, smooth_sem, rest_sem, own_sem, out_sem,
     inv_send, inv_recv, halo_send, halo_recv,
     up_send, low_recv, down_send, high_recv) = refs[24 + 4 * EXCHANGES :]

    tiles = x.shape[0]
    blocks = own.shape[0]
    rim = pack.shape[1]
    steps = tiles // GROUP
    chunk = GROUP // AGG
    g = lax.axis_index("grp")
    d = lax.axis_index("dev")

    def part(c):
        return pl.ds(c * GROUP, GROUP)

    def load(hbm, vmem, sem, c):
        return pltpu.make_async_copy(hbm.at[part(c)], vmem.at[part(c)], sem.at[c])

    for c in range(steps):
        load(rhs_hbm, rhs, rhs_sem, c).start()
        load(smooth_hbm, smooth, smooth_sem, c).start()
    for c in range(steps):
        load(jac_hbm, jac, jac_sem, c).start()
    rest_copy = pltpu.make_async_copy(rest_hbm, rest, rest_sem)
    rest_copy.start()
    own_copy = pltpu.make_async_copy(
        inv_hbm.at[0, d], inv.at[pl.ds(d * cap, cap)], own_sem
    )
    own_copy.start()

    barrier = pltpu.get_barrier_semaphore()
    for o in range(1, devs):
        pl.semaphore_signal(
            barrier, inc=1, device_id=(g, lax.rem(d + o, devs)), device_id_type=MESH
        )
    for o in range(1, grps):
        pl.semaphore_signal(
            barrier, inc=1, device_id=(lax.rem(g + o, grps), d), device_id_type=MESH
        )

    exists = (d > 0, d < devs - 1, g > 0, g < grps - 1)
    reaches = (d < devs - 1, d > 0, g < grps - 1, g > 0)
    targets = ((g, d + 1), (g, d - 1), (g + 1, d), (g - 1, d))
    for j in range(4):
        @pl.when(jnp.logical_not(exists[j]))
        def _():
            for e in range(EXCHANGES):
                ref = halos[4 * e + j]
                ref[...] = jnp.zeros_like(ref)

    @pl.when(g == 0)
    def _():
        low[...] = jnp.zeros_like(low)

    @pl.when(g == grps - 1)
    def _():
        high[...] = jnp.zeros_like(high)

    def choose(a, carry):
        mine = owners[a]
        slot = lax.fori_loop(
            0, a, lambda b, n: n + jnp.where(owners[b] == mine, 1, 0), jnp.int32(0)
        )
        pick[a] = mine * cap + slot
        return carry

    def first(c, carry):
        load(rhs_hbm, rhs, rhs_sem, c).wait()
        load(smooth_hbm, smooth, smooth_sem, c).wait()
        new = []
        for i in range(GROUP):
            t = c * GROUP + i
            new.append(OMEGA * nt(rhs[t].astype(jnp.bfloat16), smooth[t]))
        for i in range(GROUP):
            t = c * GROUP + i
            x[t] = new[i]
            u[t] = new[i].astype(jnp.bfloat16)
        return carry

    lax.fori_loop(0, steps, first, 0)
    pl.semaphore_wait(barrier, devs - 1 + grps - 1)

    def halo_copy(e, j):
        return pltpu.make_async_remote_copy(
            src_ref=pack.at[j],
            dst_ref=halos[4 * e + j],
            send_sem=halo_send.at[j],
            recv_sem=halo_recv.at[e, j],
            device_id=targets[j],
            device_id_type=MESH,
        )

    def inverse_copy(target, source):
        return pltpu.make_async_remote_copy(
            src_ref=inv_hbm.at[0, target],
            dst_ref=inv.at[pl.ds(source * cap, cap)],
            send_sem=inv_send.at[target],
            recv_sem=inv_recv.at[source],
            device_id=(g, target),
            device_id_type=MESH,
        )

    def exchange(e):
        for j in (2, 3, 0, 1):
            @pl.when(reaches[j])
            def _():
                for i in range(rim):
                    pack[j, i] = u[listed[j, i]]
                halo_copy(e, j).start()

    def arrive(e):
        for j in range(4):
            @pl.when(exists[j])
            def _():
                halo_copy(e, j).wait_recv()

            @pl.when(reaches[j])
            def _():
                halo_copy(e, j).wait_send()

    def inner(c, carry, waits):
        if waits:
            load(jac_hbm, jac, jac_sem, c).wait()
        new = []
        for i in range(GROUP):
            t = c * GROUP + i
            near = wide([u[cols[t, k]] for k in range(3)])
            new.append(rhs[t] - nt(near, wide([jac[t, k] for k in range(3)])))
        for i in range(GROUP):
            acc[c * GROUP + i] = new[i]
        return carry

    def outer(e, c):
        left = []
        for i in range(GROUP):
            t = c * GROUP + i
            far = wide([
                halos[4 * e + j][jnp.maximum(cols[t, 3 + j] - (tiles + j * rim), 0)]
                for j in range(4)
            ])
            total = acc[t] - nt(far, wide([jac[t, 3 + j] for j in range(4)]))
            left.append(total.astype(jnp.bfloat16))
        return left

    def out_copy(c):
        return pltpu.make_async_copy(x.at[part(c)], out_hbm.at[part(c)], out_sem.at[c])

    def smoothing(e, last):
        def step(c, carry):
            left = outer(e, c)
            new = []
            for i in range(GROUP):
                t = c * GROUP + i
                new.append(x[t] + OMEGA * nt(left[i], smooth[t]))
            for i in range(GROUP):
                t = c * GROUP + i
                x[t] = new[i]
                if not last:
                    u[t] = new[i].astype(jnp.bfloat16)
            if last:
                out_copy(c).start()
            return carry

        return step

    def near_part(e):
        exchange(e)
        if e == 0:
            for o in range(1, devs):
                inverse_copy(lax.rem(d + o, devs), d).start()
            lax.fori_loop(0, blocks, choose, 0)
        lax.fori_loop(0, steps, functools.partial(inner, waits=e == 0), 0)
        arrive(e)

    for e in range(SWEEPS - 1):
        near_part(e)
        lax.fori_loop(0, steps, smoothing(e, False), 0)

    near_part(SWEEPS - 1)
    rest_copy.wait()
    in_low = g < grps // 2
    in_high = jnp.logical_not(in_low)
    edge = jnp.logical_or(g == 0, g == grps - 1)

    def some(c):
        return pl.ds(c * chunk, chunk)

    def up_copy(c):
        return pltpu.make_async_remote_copy(
            src_ref=up.at[some(c)],
            dst_ref=low.at[some(c)],
            send_sem=up_send.at[c],
            recv_sem=low_recv.at[c],
            device_id=(g + 1, d),
            device_id_type=MESH,
        )

    def down_copy(c):
        return pltpu.make_async_remote_copy(
            src_ref=down.at[some(c)],
            dst_ref=high.at[some(c)],
            send_sem=down_send.at[c],
            recv_sem=high_recv.at[c],
            device_id=(g - 1, d),
            device_id_type=MESH,
        )

    def send_up(c):
        up[some(c)] = (low[some(c)].astype(jnp.float32) + own[some(c)]).astype(jnp.bfloat16)
        up_copy(c).start()

    def send_down(c):
        down[some(c)] = (high[some(c)].astype(jnp.float32) + own[some(c)]).astype(jnp.bfloat16)
        down_copy(c).start()

    def forward(c):
        @pl.when(in_low)
        def _():
            @pl.when(g > 0)
            def _():
                up_copy(c).wait_recv()

            send_up(c)

        @pl.when(in_high)
        def _():
            @pl.when(g < grps - 1)
            def _():
                down_copy(c).wait_recv()

            send_down(c)

    def finish(c):
        @pl.when(in_low)
        def _():
            down_copy(c).wait_recv()

            @pl.when(g > 0)
            def _():
                send_down(c)

        @pl.when(in_high)
        def _():
            up_copy(c).wait_recv()

            @pl.when(g < grps - 1)
            def _():
                send_up(c)

    def restrict(c, carry):
        left = outer(SWEEPS - 1, c)
        new = []
        for i in range(chunk):
            t = c * GROUP + AGG * i
            new.append(nt(wide([left[AGG * i + k] for k in range(AGG)]),
                          wide([rest[t + k] for k in range(AGG)])))
        for i in range(chunk):
            own[c * chunk + i] = new[i]

        @pl.when(edge)
        def _():
            forward(c)

        @pl.when(jnp.logical_and(jnp.logical_not(edge), c >= LAG))
        def _():
            forward(c - LAG)

        return carry

    lax.fori_loop(0, steps, restrict, 0)

    @pl.when(jnp.logical_not(edge))
    def _():
        for c in range(steps - LAG, steps):
            forward(c)

    own_copy.wait()
    for o in range(1, devs):
        inverse_copy(lax.rem(d + o, devs), lax.rem(d + devs - o, devs)).wait()

    def correct(c, carry):
        finish(c)
        fixes = []
        for i in range(chunk):
            a = c * chunk + i
            whole = low[a].astype(jnp.float32) + own[a] + high[a].astype(jnp.float32)
            fixes.append(nt(whole.astype(jnp.bfloat16), inv[pick[a]]).astype(jnp.bfloat16))
        new = []
        for i in range(chunk):
            t = c * GROUP + AGG * i
            both = jnp.dot(
                fixes[i], wide([rest[t + k] for k in range(AGG)]),
                preferred_element_type=jnp.float32,
            )
            width = both.shape[1] // AGG
            for k in range(AGG):
                new.append(x[t + k] + both[:, k * width : (k + 1) * width])
        for i in range(GROUP):
            t = c * GROUP + i
            x[t] = new[i]
            u[t] = new[i].astype(jnp.bfloat16)
        return carry

    lax.fori_loop(0, steps, correct, 0)

    for e in range(SWEEPS, 2 * SWEEPS):
        near_part(e)
        lax.fori_loop(0, steps, smoothing(e, e == 2 * SWEEPS - 1), 0)

    for c in range(steps):
        @pl.when(g < grps - 1)
        def _():
            up_copy(c).wait_send()

        @pl.when(g > 0)
        def _():
            down_copy(c).wait_send()

        out_copy(c).wait()


def shards(rhs, jacobian, columns, send_tiles, smoother, restriction, coarse_inverse, owner):
    grps, devs = lax.axis_size("grp"), lax.axis_size("dev")
    tiles, vectors, rows = rhs.shape
    blocks = tiles // AGG
    cap = coarse_inverse.shape[2]
    rim = send_tiles.shape[2]
    steps = tiles // GROUP
    mine = lax.dynamic_slice_in_dim(owner[:, 0], lax.axis_index("dev") * blocks, blocks)
    bf, f32 = jnp.bfloat16, jnp.float32
    dma = pltpu.SemaphoreType.DMA
    smem = pl.BlockSpec(memory_space=pltpu.SMEM)
    hbm = pl.BlockSpec(memory_space=pl.ANY)
    coarse = (blocks, vectors, rows)
    return pl.pallas_call(
        functools.partial(kernel, (grps, devs, cap)),
        out_shape=jax.ShapeDtypeStruct(rhs.shape, f32),
        in_specs=[smem] * 3 + [hbm] * 5,
        out_specs=hbm,
        scratch_shapes=[
            pltpu.VMEM(rhs.shape, f32),
            pltpu.VMEM(jacobian.shape, bf),
            pltpu.VMEM(smoother.shape, bf),
            pltpu.VMEM(restriction.shape, bf),
            pltpu.VMEM((devs * cap, rows, rows), bf),
            pltpu.VMEM(rhs.shape, f32),
            pltpu.VMEM(rhs.shape, f32),
            pltpu.VMEM(rhs.shape, bf),
            pltpu.VMEM((4, rim, vectors, rows), bf),
            pltpu.VMEM(coarse, f32),
            pltpu.VMEM(coarse, bf),
            pltpu.VMEM(coarse, bf),
            pltpu.VMEM(coarse, bf),
            pltpu.VMEM(coarse, bf),
            pltpu.SMEM((blocks,), jnp.int32),
            *[pltpu.VMEM((rim, vectors, rows), bf) for _ in range(4 * EXCHANGES)],
            dma((steps,)),
            dma((steps,)),
            dma((steps,)),
            dma,
            dma,
            dma((steps,)),
            dma((devs,)),
            dma((devs,)),
            dma((4,)),
            dma((EXCHANGES, 4)),
            dma((steps,)),
            dma((steps,)),
            dma((steps,)),
            dma((steps,)),
        ],
        compiler_params=pltpu.CompilerParams(
            collective_id=0, has_side_effects=True, vmem_limit_bytes=56 * 1024 * 1024
        ),
    )(columns, send_tiles[0], mine, rhs, jacobian, smoother, restriction, coarse_inverse)


def solution(mesh):
    in_specs = (
        P(("grp", "dev"), None, None),
        P(("grp", "dev"), None, None, None),
        P(("grp", "dev"), None),
        P(("grp", "dev"), None, None),
        P(("grp", "dev"), None, None),
        P(("grp", "dev"), None, None),
        P("dev", None, None, None, None),
        P(),
    )
    out_specs = P(("grp", "dev"), None, None)
    return jax.shard_map(shards, mesh=mesh, in_specs=in_specs, out_specs=out_specs, check_vma=False)
```
